512 devices in a mesh: replica: 8 (over x, core), shard: 16 (over z), tensor: 4 (over y).
Axes of the slice: x: 4, y: 4, z: 16, core: 2. Of those that a mesh axis runs over, the one named last changes fastest.
Arguments:
- gradients: bfloat16 [8, 64, 512, 512], P('replica', None, ('shard', 'tensor')), may hold values from -2 to 2
- old_stats: float32 [128, 2, 512, 512], P(('shard', 'tensor'), None, 'replica'), as said below
- owner_slot: int32 [64], replicated, may hold values from 0 to 127, as said below
Outputs:
- updates: bfloat16 [64, 512, 512], P(None, ('shard', 'tensor'))
The draws below stay inside these ranges and needn't reach their ends.
Inputs may be any that keep to these rules, and one draw needn't show every extreme that they name: `old_stats`: symmetric positive definite in every slot and side. `owner_slot`: values are distinct; some owner holds 2 blocks.
All inputs are finite; a program needn't handle non-finite values.
Results may differ from the reference program's by a relative error of at most 0.02.
Values may be sent and summed in bfloat16 or wider, within the bound.
No kernel may reach another device: no remote copies, remote signals or barrier semaphores. Data moves between devices by JAX's collectives and lax.ppermute only.
A program may use at most 64 MiB of HBM per device.

```python
import math
import jax
import jax.numpy as jnp
from jax import lax

BLK = 512
NEWTON = 2
REPS = 8
OWNERS = 64
SLOTS = 2
BLOCKS = 64


def draw_old_stats(key, part):
    key = jax.random.fold_in(key, 23)
    first_key, second_key = jax.random.split(key)
    lead_shape = (OWNERS * SLOTS, 2, BLK)
    reach = 2.0
    scale_low = 0.3
    scale_high = 3.0
    ridge_share = 0.3
    positions = jax.random.uniform(first_key, lead_shape, jnp.float32, 0.0, 1.0)
    squared_scales = jnp.exp(jax.random.uniform(second_key, lead_shape, jnp.float32, math.log(scale_low), math.log(scale_high)))
    row_scales = jnp.sqrt(squared_scales)
    kernel = jnp.exp(-jnp.abs(positions[..., :, None] - positions[..., None, :]) * (BLK / reach))
    identity = jnp.eye(BLK, dtype=jnp.float32)
    mixed = (kernel + ridge_share * identity) * row_scales[..., :, None] * row_scales[..., None, :]
    return BLK * mixed


def draw_owner_slot(key, part):
    key = jax.random.fold_in(key, 11)
    first_key, second_key, third_key = jax.random.split(key, 3)
    slot_total = OWNERS * SLOTS
    slot_rank = jax.random.permutation(first_key, slot_total).astype(jnp.int32)
    full_owner = jax.random.randint(second_key, (), 0, OWNERS)
    within = jnp.arange(SLOTS, dtype=jnp.int32)
    scores = slot_rank.at[full_owner * SLOTS + within].set(within - SLOTS - 2)
    scores = scores.at[0].set(-2).at[slot_total - 1].set(-1)
    chosen = jnp.argsort(scores)[:BLOCKS]
    shuffle = jax.random.permutation(third_key, BLOCKS)
    return chosen[shuffle].astype(jnp.int32)


def levels(own_key, shape, cuts, least, top_value):
    def one(dim, blocks):
        steps = jax.random.uniform(jax.random.fold_in(jax.random.fold_in(own_key, 6), dim), (blocks,), jnp.float32, least / len(cuts), top_value / len(cuts))
        return jnp.repeat(jnp.exp(steps), shape[dim] // blocks).reshape((-1,) + (1,) * (len(shape) - dim - 1))

    level = one(*cuts[0])
    for cut in cuts[1:]:
        level = level * one(*cut)
    return level


def bell_draw(stream_key, dims, scale, most, cuts=(), held_as=jnp.bfloat16):
    entries = scale * jax.random.normal(stream_key, dims, jnp.float32)
    if cuts:
        entries = entries * levels(stream_key, dims, cuts, -0.22, 0.18)
    return jnp.clip(entries, -most, most).astype(held_as)


def setup_inputs(seed: int = 0) -> dict:
    splits = jax.random.split(jax.random.key(seed), 4)
    return {
        "gradients": bell_draw(splits[0], (REPS, BLOCKS, BLK, BLK), REPS ** -0.5, 2.0, ((0, 8), (2, 64))),
        "old_stats": draw_old_stats(jax.random.fold_in(splits[3], 71), 0),
        "owner_slot": draw_owner_slot(jax.random.fold_in(splits[3], 71), 0),
    }


ridge_term = 1e-06
decay_rate = 0.95
graft_floor = 1e-06
start_scale = 4.0

def product(left, right):
    return jnp.einsum('nij,njk->nik', left.astype(jnp.float32), right.astype(jnp.float32), precision=lax.Precision.HIGHEST)

def inverse_root(matrices):
    identity = jnp.eye(BLK, dtype=jnp.float32)
    shifted = matrices + ridge_term * identity
    norm_size = jnp.sqrt(lax.optimization_barrier(jnp.sum(shifted * shifted, axis=(1, 2), keepdims=True)))
    iterate = start_scale * shifted / norm_size
    root_now = None
    for newton_step in range(NEWTON):
        factor = ((5.0 * identity - iterate) / 4.0).astype(jnp.bfloat16)
        if newton_step == 0:
            root_now = factor
        else:
            root_now = product(root_now, factor).astype(jnp.bfloat16)
        if newton_step + 1 < NEWTON:
            square = product(factor, factor).astype(jnp.bfloat16)
            fourth = product(square, square).astype(jnp.bfloat16)
            iterate = product(fourth, iterate.astype(jnp.bfloat16))
    return root_now

def reference(gradients, old_stats, owner_slot):
    grad_sum = lax.optimization_barrier(jnp.sum(gradients.astype(jnp.float32), axis=0))

    def one_block(pair):
        block_sum, slot_index = pair
        previous = lax.dynamic_index_in_dim(old_stats, slot_index.astype(jnp.int32), 0, keepdims=False)
        grad_low = block_sum.astype(jnp.bfloat16)
        left_stat = decay_rate * previous[0] + jnp.dot(grad_low, grad_low.T, preferred_element_type=jnp.float32)
        right_stat = decay_rate * previous[1] + jnp.dot(grad_low.T, grad_low, preferred_element_type=jnp.float32)
        root_pair = inverse_root(jnp.stack([left_stat, right_stat]))
        half_product = jnp.dot(root_pair[0], grad_low, preferred_element_type=jnp.float32).astype(jnp.bfloat16)
        precond = jnp.dot(half_product, root_pair[1], preferred_element_type=jnp.float32)
        mean_grad = jnp.mean(block_sum * block_sum)
        mean_pre = jnp.mean(precond * precond)
        return (precond * jnp.sqrt(mean_grad) / jnp.sqrt(mean_pre + graft_floor)).astype(jnp.bfloat16)
    return lax.map(one_block, (grad_sum, owner_slot))
```

```python
import jax
import jax.numpy as jnp
from jax import lax
from jax.experimental import pallas as pl
from jax.experimental.pallas import tpu as pltpu
from jax.sharding import Mesh, PartitionSpec as P

ridge_term = 1e-06
decay_rate = 0.95
graft_floor = 1e-06
start_scale = 4.0

BF = jnp.bfloat16
F32 = jnp.float32
VMEM_LIMIT = 48 * 1024 * 1024


def call(kernel, out_shape, in_kinds, scratch=(), flops=0, nbytes=1 << 20):
    kinds = {"v": pltpu.VMEM, "s": pltpu.SMEM}
    single = not isinstance(out_shape, (list, tuple))
    spec = pl.BlockSpec(memory_space=pltpu.VMEM)
    return pl.pallas_call(
        kernel,
        out_shape=out_shape,
        in_specs=[pl.BlockSpec(memory_space=kinds[k]) for k in in_kinds],
        out_specs=spec if single else [spec] * len(out_shape),
        scratch_shapes=list(scratch),
        compiler_params=pltpu.CompilerParams(vmem_limit_bytes=VMEM_LIMIT),
        cost_estimate=pl.CostEstimate(flops=flops, bytes_accessed=nbytes, transcendentals=0),
    )


def place_kernel(ny, nz, slot_ref, core_ref, grad_ref, stat_ref, keep_ref, send_ref):
    blocks = grad_ref.shape[0]
    owners = ny * nz
    core = core_ref[0]
    keep_ref[:owners] = jnp.zeros((owners,) + keep_ref.shape[1:], BF)
    send_ref[:owners] = jnp.zeros((owners,) + keep_ref.shape[1:], BF)

    def step(block, carry):
        slot = slot_ref[block]
        owner = slot // 2
        place = (owner % ny) * nz + owner // ny
        mine = slot % 2 == core

        @pl.when(mine)
        def _():
            keep_ref[place] = grad_ref[block]

        @pl.when(jnp.logical_not(mine))
        def _():
            send_ref[place] = grad_ref[block]

        return carry

    lax.fori_loop(0, blocks, step, 0, unroll=4)
    tail = keep_ref.shape[0] - owners
    tail_shape = (tail,) + keep_ref.shape[1:]
    keep_ref[owners:] = stat_ref[core].reshape(tail_shape).astype(BF)
    send_ref[owners:] = stat_ref[1 - core].reshape(tail_shape).astype(BF)


def quarter_kernel(nx, core_ref, keep_ref, got_ref, out_ref, stat_ref):
    owners = out_ref.shape[1] * out_ref.shape[2]
    width = out_ref.shape[-1]
    core = core_ref[0]
    for part in range(nx):
        cols = slice(part * width, (part + 1) * width)
        total = keep_ref[:owners, :, cols].astype(F32) + got_ref[:owners, :, cols].astype(F32)
        out_ref[part] = total.astype(BF).reshape(out_ref.shape[1:])
    stat_ref[core] = keep_ref[owners:]
    stat_ref[1 - core] = got_ref[owners:]


def sum_kernel(in_ref, out_ref):
    nx, ny = in_ref.shape[:2]
    for part in range(ny):
        total = in_ref[0, part].astype(F32)
        for copy in range(1, nx):
            total = total + in_ref[copy, part].astype(F32)
        out_ref[:, part] = total.astype(BF)


def dot(left, right, contract=((1,), (0,))):
    return lax.dot_general(left, right, (contract, ((), ())), preferred_element_type=F32)


def step_kernel(nx, place_ref, quarter_ref, *refs):
    stat_refs, (out_ref, grad_ref, stats) = refs[:nx], refs[nx:]
    order = grad_ref.shape[0]
    width = quarter_ref.shape[-1]
    rows = order // nx
    x = place_ref[1]
    for part in range(nx):
        grad_ref[:, part * width : (part + 1) * width] = quarter_ref[part]
    for shift in range(nx):
        source = lax.rem(x - shift + nx, nx)
        for core in range(2):
            start = pl.multiple_of(source * rows + core * (rows // 2), rows // 2)
            for side in range(2):
                stats[side, pl.ds(start, rows // 2), :] = stat_refs[shift][core, side]
    grad = grad_ref[...]
    row_ids = lax.broadcasted_iota(jnp.int32, (order, order), 0)
    col_ids = lax.broadcasted_iota(jnp.int32, (order, order), 1)
    diagonal = row_ids == col_ids
    roots = []
    for side in range(2):
        gram = dot(grad, grad, ((1,), (1,)) if side == 0 else ((0,), (0,)))
        shifted = decay_rate * stats[side].astype(F32) + gram + jnp.where(diagonal, ridge_term, 0.0)
        scale = start_scale * lax.rsqrt(jnp.sum(shifted * shifted))
        iterate = shifted * scale
        factor = (jnp.where(diagonal, 1.25, 0.0) - 0.25 * iterate).astype(BF)
        square = dot(factor, factor).astype(BF)
        fourth = dot(square, square).astype(BF)
        iterate = dot(fourth, iterate.astype(BF))
        second = (jnp.where(diagonal, 1.25, 0.0) - 0.25 * iterate).astype(BF)
        roots.append(dot(factor, second).astype(BF))
    half = dot(roots[0], grad).astype(BF)
    precond = dot(half, roots[1])
    count = float(order * order)
    grad32 = grad.astype(F32)
    mean_grad = jnp.sum(grad32 * grad32) / count
    mean_pre = jnp.sum(precond * precond) / count
    scale = jnp.sqrt(mean_grad) / jnp.sqrt(mean_pre + graft_floor)
    for part in range(nx):

        @pl.when(x == part)
        def _():
            out_ref[...] = (precond[:, part * width : (part + 1) * width] * scale).astype(BF)


def spread_kernel(in_ref, out_ref):
    nx, ny = out_ref.shape[:2]
    for part in range(ny):
        piece = in_ref[:, part]
        for copy in range(nx):
            out_ref[copy, part] = piece


def pick_kernel(ny, slot_ref, core_ref, own_ref, got_ref, out_ref):
    nx = own_ref.shape[0]
    width = own_ref.shape[-1]
    core = core_ref[0]

    def step(block, carry):
        slot = slot_ref[block]
        owner = slot // 2
        y, z = owner % ny, owner // ny
        mine = slot % 2 == core

        @pl.when(mine)
        def _():
            for part in range(nx):
                out_ref[block, :, part * width : (part + 1) * width] = own_ref[part, y, z]

        @pl.when(jnp.logical_not(mine))
        def _():
            for part in range(nx):
                out_ref[block, :, part * width : (part + 1) * width] = got_ref[part, y, z]

        return carry

    lax.fori_loop(0, out_ref.shape[0], step, 0, unroll=4)


def shaped(shape, dtype=BF):
    return jax.ShapeDtypeStruct(shape, dtype)


def on_device(gradients, old_stats, owner_slot):
    nx, nz, ny = lax.axis_size("x"), lax.axis_size("shard"), lax.axis_size("tensor")
    grads = gradients[0]
    blocks, rows, order = grads.shape
    owners = ny * nz
    width = order // nx
    stat_rows = old_stats.shape[2]
    tail = 2 * stat_rows // rows
    here = jnp.stack([lax.axis_index("core"), lax.axis_index("x")]).astype(jnp.int32)
    swap = [(0, 1), (1, 0)]

    def place(*refs):
        place_kernel(ny, nz, *refs)

    whole = (owners + tail, rows, order)
    keep, send = call(place, [shaped(whole), shaped(whole)], "ssvv")(owner_slot, here, grads, old_stats)
    got = lax.ppermute(send, "core", swap)

    def quarter(*refs):
        quarter_kernel(nx, *refs)

    parts, stat = call(
        quarter, [shaped((nx, ny, nz, rows, width)), shaped((2, tail, rows, order))], "svv"
    )(here, keep, got)
    parts = lax.all_to_all(
        parts.reshape(nx * ny, nz, rows, width), ("x", "tensor"), split_axis=0, concat_axis=0, tiled=True
    ).reshape(nx, ny, nz, rows, width)
    stat = stat.reshape(2, 2, stat_rows, order)
    stats = [stat] + [
        lax.ppermute(stat, "x", [(i, (i + shift) % nx) for i in range(nx)]) for shift in range(1, nx)
    ]
    summed = call(sum_kernel, shaped((nz, ny, rows, width)), "v")(parts)
    quarter_grad = lax.all_to_all(summed, "shard", split_axis=0, concat_axis=0, tiled=True)
    quarter_grad = quarter_grad.reshape(1, order, width)
    quarters = lax.all_to_all(
        jnp.broadcast_to(quarter_grad, (nx, order, width)), "x", split_axis=0, concat_axis=0, tiled=True
    )

    def step(*refs):
        step_kernel(nx, *refs)

    update = call(
        step,
        shaped((order, width)),
        "sv" + "v" * nx,
        scratch=[pltpu.VMEM((order, order), BF), pltpu.VMEM((2, order, order), BF)],
        flops=24 * order**3,
        nbytes=2 << 20,
    )(here, quarters, *stats)
    back = lax.all_to_all(
        update.reshape(nz, ny, rows, width), "shard", split_axis=0, concat_axis=0, tiled=True
    )
    spread = call(spread_kernel, shaped((nx, ny, nz, rows, width)), "v")(back)
    own = lax.all_to_all(
        spread.reshape(nx * ny, nz, rows, width), ("x", "tensor"), split_axis=0, concat_axis=0, tiled=True
    ).reshape(nx, ny, nz, rows, width)
    other = lax.ppermute(own, "core", swap)

    def pick(*refs):
        pick_kernel(ny, *refs)

    return call(pick, shaped((blocks, rows, order)), "ssvv")(owner_slot, here, own, other)


def solution(mesh):
    replica, nz, ny = (mesh.shape[name] for name in ("replica", "shard", "tensor"))
    fine = Mesh(mesh.devices.reshape(replica // 2, 2, nz, ny), ("x", "core", "shard", "tensor"))
    replicas, rows = ("x", "core"), ("shard", "tensor")
    return jax.shard_map(
        on_device,
        mesh=fine,
        in_specs=(P(replicas, None, rows, None), P(rows, None, replicas, None), P()),
        out_specs=P(None, rows, None),
        check_vma=False,
    )
```

```python
import functools

import jax
import jax.numpy as jnp
from jax import lax
from jax.experimental import pallas as pl
from jax.experimental.pallas import tpu as pltpu
from jax.sharding import Mesh, PartitionSpec as P

ridge_term = 1e-06
decay_rate = 0.95
graft_floor = 1e-06
start_scale = 4.0

BF = jnp.bfloat16
F32 = jnp.float32
VMEM_LIMIT = 48 * 1024 * 1024


def call(kernel, out_shape, in_kinds, scratch=(), out_kind="v", flops=0, nbytes=1 << 20):
    kinds = {"v": pltpu.VMEM, "h": pltpu.HBM}
    single = not isinstance(out_shape, (list, tuple))
    spec = pl.BlockSpec(memory_space=kinds[out_kind])
    return pl.pallas_call(
        kernel,
        out_shape=out_shape,
        in_specs=[pl.BlockSpec(memory_space=kinds[k]) for k in in_kinds],
        out_specs=spec if single else [spec] * len(out_shape),
        scratch_shapes=list(scratch),
        compiler_params=pltpu.CompilerParams(vmem_limit_bytes=VMEM_LIMIT),
        cost_estimate=pl.CostEstimate(flops=flops, bytes_accessed=nbytes, transcendentals=0),
    )


def place_kernel(ny, nz, slot_hbm, grad_hbm, stat_hbm, keep_ref, send_ref, slots, source, grads, stats, sems):
    blocks = grad_hbm.shape[1]
    owners = ny * nz
    core = lax.axis_index("core")
    copies = [
        pltpu.make_async_copy(slot_hbm, slots, sems.at[0]),
        pltpu.make_async_copy(grad_hbm.at[0], grads.at[pl.ds(0, blocks)], sems.at[1]),
        pltpu.make_async_copy(stat_hbm, stats, sems.at[2]),
    ]
    for copy in copies:
        copy.start()
    grads[blocks] = jnp.zeros(grads.shape[1:], BF)

    def clear(place, carry):
        source[place] = blocks
        return carry

    lax.fori_loop(0, 2 * owners, clear, 0, unroll=8)
    copies[0].wait()

    def fill(block, carry):
        slot = slots[block]
        owner = slot // 2
        away = (slot % 2 + core) % 2
        source[away * owners + (owner % ny) * nz + owner // ny] = block
        return carry

    lax.fori_loop(0, blocks, fill, 0, unroll=8)
    copies[1].wait()

    def move(place, carry):
        keep_ref[place] = grads[source[place]]
        send_ref[place] = grads[source[owners + place]]
        return carry

    lax.fori_loop(0, owners, move, 0, unroll=8)
    copies[2].wait()
    tail_shape = (keep_ref.shape[0] - owners,) + keep_ref.shape[1:]
    keep_ref[owners:] = stats[core].reshape(tail_shape).astype(BF)
    send_ref[owners:] = stats[1 - core].reshape(tail_shape).astype(BF)


def quarter_kernel(nx, keep_ref, got_ref, out_ref, stat_ref):
    owners = out_ref.shape[1] * out_ref.shape[2]
    width = out_ref.shape[-1]
    core = lax.axis_index("core")
    for part in range(nx):
        cols = slice(part * width, (part + 1) * width)
        total = keep_ref[:owners, :, cols].astype(F32) + got_ref[:owners, :, cols].astype(F32)
        out_ref[part] = total.astype(BF).reshape(out_ref.shape[1:])
    half = stat_ref.shape[1] // 2
    for ref, place in ((keep_ref, core), (got_ref, 1 - core)):
        rows = pl.ds(pl.multiple_of(place * half, half), half)
        stat_ref[:, rows, :] = ref[owners:].reshape(2, half, stat_ref.shape[2])


def sum_kernel(in_ref, out_ref):
    nx, ny = in_ref.shape[:2]
    for part in range(ny):
        total = in_ref[0, part].astype(F32)
        for copy in range(1, nx):
            total = total + in_ref[copy, part].astype(F32)
        out_ref[:, part] = total.astype(BF)


def fan_kernel(in_ref, stat_ref, out_ref):
    nx = out_ref.shape[0]
    order, width = in_ref.shape
    x = lax.axis_index("x")

    def columns(side, shift):
        return stat_ref[side, :, pl.ds(pl.multiple_of(lax.rem(x + shift, nx) * width, width), width)]

    for chip in range(nx):
        out_ref[chip, :order] = in_ref[...]
    for shift in range(1, nx):
        chip = lax.rem(x - shift + nx, nx)
        for side in range(2):
            base = order + 2 * side * width
            out_ref[chip, base : base + width] = columns(side, 0)
            out_ref[chip, base + width : base + 2 * width] = columns(side, 1 if shift < nx - 1 else 2)


def dot(left, right, contract=((1,), (0,))):
    return lax.dot_general(left, right, (contract, ((), ())), preferred_element_type=F32)


def step_kernel(own_ref, got_ref, out_ref, grad_ref, stat_ref):
    nx, _, width = got_ref.shape
    order = grad_ref.shape[0]
    x = lax.axis_index("x")
    for part in range(nx):
        grad_ref[:, part * width : (part + 1) * width] = got_ref[part, :order]

    eye = (
        lax.broadcasted_iota(jnp.int32, (width, width), 0) == lax.broadcasted_iota(jnp.int32, (width, width), 1)
    ).astype(BF)

    def at(shift):
        return pl.ds(pl.multiple_of(lax.rem(x + shift, nx) * width, width), width)

    for side in range(2):
        stat_ref[side, at(0), :] = own_ref[side]
        for shift in range(1, nx):
            block = own_ref[side, :, at(shift)]
            stat_ref[side, at(shift), at(0)] = dot(eye, block, ((1,), (1,))).astype(BF)
            source = lax.rem(x + shift, nx)
            partner = shift % (nx - 1) + 1
            base = order + 2 * side * width
            stat_ref[side, at(shift), at(shift)] = got_ref[source, base : base + width]
            block = got_ref[source, base + width : base + 2 * width]
            stat_ref[side, at(shift), at(partner)] = block
            stat_ref[side, at(partner), at(shift)] = dot(eye, block, ((1,), (1,))).astype(BF)

    grad = grad_ref[...]
    row_ids = lax.broadcasted_iota(jnp.int32, (order, order), 0)
    col_ids = lax.broadcasted_iota(jnp.int32, (order, order), 1)
    diagonal = row_ids == col_ids
    roots = []
    for side in range(2):
        gram = dot(grad, grad, ((1,), (1,)) if side == 0 else ((0,), (0,)))
        shifted = decay_rate * stat_ref[side].astype(F32) + gram + jnp.where(diagonal, ridge_term, 0.0)
        delta = shifted * (-0.25 * start_scale * lax.rsqrt(jnp.sum(shifted * shifted)))
        low = delta.astype(BF)
        squared = dot(low, low)
        square = (squared + 2.5 * delta + jnp.where(diagonal, 1.5625, 0.0)).astype(BF)
        tail = (1.25 * delta + squared).astype(BF)
        fourth = dot(square, square).astype(BF)
        root = dot(fourth, tail) + 1.25 * delta + jnp.where(diagonal, 1.5625, 0.0)
        roots.append(root.astype(BF))
    half = dot(roots[0], grad).astype(BF)
    precond = dot(half, roots[1])
    count = float(order * order)
    grad32 = grad.astype(F32)
    mean_grad = jnp.sum(grad32 * grad32) / count
    mean_pre = jnp.sum(precond * precond) / count
    scale = jnp.sqrt(mean_grad) / jnp.sqrt(mean_pre + graft_floor)
    for part in range(nx):

        @pl.when(x == part)
        def _():
            out_ref[...] = (precond[:, part * width : (part + 1) * width] * scale).astype(BF)


def spread_kernel(in_ref, out_ref):
    nx, ny = out_ref.shape[:2]
    for part in range(ny):
        piece = in_ref[:, part]
        for copy in range(nx):
            out_ref[copy, part] = piece


def pick_kernel(chunks, slot_hbm, own_ref, got_ref, out_hbm, slots, out, sems):
    nx, ny, nz = own_ref.shape[:3]
    width = own_ref.shape[-1]
    blocks = out.shape[0]
    size = blocks // chunks
    core = lax.axis_index("core")
    fetch = pltpu.make_async_copy(slot_hbm, slots, sems.at[chunks])
    fetch.start()
    fetch.wait()
    copies = []
    for chunk in range(chunks):

        def move(step, carry):
            block = chunk * size + step
            slot = slots[block]
            owner = slot // 2
            y, z = owner % ny, owner // ny
            mine = slot % 2 == core
            for part in range(nx):
                out[block, :, part * width : (part + 1) * width] = jnp.where(
                    mine, own_ref[part, y, z], got_ref[part, y, z]
                )
            return carry

        lax.fori_loop(0, size, move, 0, unroll=8)
        span = pl.ds(chunk * size, size)
        copies.append(pltpu.make_async_copy(out.at[span], out_hbm.at[span], sems.at[chunk]))
        copies[-1].start()
    for copy in copies:
        copy.wait()


def shaped(shape, dtype=BF):
    return jax.ShapeDtypeStruct(shape, dtype)


def on_device(gradients, old_stats, owner_slot):
    nx, nz, ny = lax.axis_size("x"), lax.axis_size("shard"), lax.axis_size("tensor")
    blocks, rows, order = gradients.shape[1:]
    owners = ny * nz
    width = order // nx
    stat_rows = old_stats.shape[2]
    tail = 2 * stat_rows // rows
    swap = [(0, 1), (1, 0)]
    exchange = functools.partial(lax.all_to_all, split_axis=0, concat_axis=0, tiled=True)

    whole = (owners + tail, rows, order)
    keep, send = call(
        functools.partial(place_kernel, ny, nz),
        [shaped(whole), shaped(whole)],
        "hhh",
        scratch=[
            pltpu.SMEM(owner_slot.shape, jnp.int32),
            pltpu.SMEM((2 * owners,), jnp.int32),
            pltpu.VMEM((blocks + 1, rows, order), BF),
            pltpu.VMEM(old_stats.shape, F32),
            pltpu.SemaphoreType.DMA((3,)),
        ],
    )(owner_slot, gradients, old_stats)
    got = lax.ppermute(send, "core", swap)
    parts, stat = call(
        functools.partial(quarter_kernel, nx),
        [shaped((nx, ny, nz, rows, width)), shaped((2, 2 * stat_rows, order))],
        "vv",
    )(keep, got)
    parts = exchange(parts.reshape(nx * ny, nz, rows, width), ("x", "tensor"))
    summed = call(sum_kernel, shaped((nz, ny, rows, width)), "v")(parts.reshape(nx, ny, nz, rows, width))
    quarter_grad = exchange(summed, "shard").reshape(order, width)
    fanned = call(fan_kernel, shaped((nx, order + 4 * width, width)), "vv")(quarter_grad, stat)
    gathered = exchange(fanned, "x")
    update = call(
        step_kernel,
        shaped((order, width)),
        "vv",
        scratch=[pltpu.VMEM((order, order), BF), pltpu.VMEM((2, order, order), BF)],
        flops=20 * order**3,
        nbytes=2 << 20,
    )(stat, gathered)
    back = exchange(update.reshape(nz, ny, rows, width), "shard")
    spread = call(spread_kernel, shaped((nx, ny, nz, rows, width)), "v")(back)
    own = exchange(spread.reshape(nx * ny, nz, rows, width), ("x", "tensor"))
    own = own.reshape(nx, ny, nz, rows, width)
    chunks = 4
    return call(
        functools.partial(pick_kernel, chunks),
        shaped((blocks, rows, order)),
        "hvv",
        scratch=[
            pltpu.SMEM(owner_slot.shape, jnp.int32),
            pltpu.VMEM((blocks, rows, order), BF),
            pltpu.SemaphoreType.DMA((chunks + 1,)),
        ],
        out_kind="h",
    )(owner_slot, own, lax.ppermute(own, "core", swap))


def solution(mesh):
    replica, nz, ny = (mesh.shape[name] for name in ("replica", "shard", "tensor"))
    fine = Mesh(mesh.devices.reshape(replica // 2, 2, nz, ny), ("x", "core", "shard", "tensor"))
    replicas, rows = ("x", "core"), ("shard", "tensor")
    return jax.shard_map(
        on_device,
        mesh=fine,
        in_specs=(P(replicas, None, rows, None), P(rows, None, replicas, None), P()),
        out_specs=P(None, rows, None),
        check_vma=False,
    )
```

```python
import functools

import jax
import jax.numpy as jnp
from jax import lax
from jax.experimental import pallas as pl
from jax.experimental.pallas import tpu as pltpu
from jax.sharding import Mesh, PartitionSpec as P

ridge_term = 1e-06
decay_rate = 0.95
graft_floor = 1e-06
start_scale = 4.0

BF = jnp.bfloat16
F32 = jnp.float32
VMEM_LIMIT = 48 * 1024 * 1024


def call(kernel, out_shape, in_kinds, scratch=(), out_kind="v", flops=0, nbytes=1 << 20):
    kinds = {"v": pltpu.VMEM, "h": pltpu.HBM}
    single = not isinstance(out_shape, (list, tuple))
    spec = pl.BlockSpec(memory_space=kinds[out_kind])
    return pl.pallas_call(
        kernel,
        out_shape=out_shape,
        in_specs=[pl.BlockSpec(memory_space=kinds[k]) for k in in_kinds],
        out_specs=spec if single else [spec] * len(out_shape),
        scratch_shapes=list(scratch),
        compiler_params=pltpu.CompilerParams(vmem_limit_bytes=VMEM_LIMIT),
        cost_estimate=pl.CostEstimate(flops=flops, bytes_accessed=nbytes, transcendentals=0),
    )


def place_kernel(ny, nz, chunks, slot_hbm, grad_hbm, stat_hbm, keep_ref, send_ref, slots, grads, stats, sems):
    blocks = grads.shape[0]
    owners = ny * nz
    dump = keep_ref.shape[0] - 1
    size = blocks // chunks
    core = lax.axis_index("core")
    fetch = pltpu.make_async_copy(slot_hbm, slots, sems.at[chunks])
    fetch.start()
    copies = []
    for chunk in range(chunks):
        span = pl.ds(chunk * size, size)
        copies.append(pltpu.make_async_copy(grad_hbm.at[0, span], grads.at[span], sems.at[chunk]))
        copies[-1].start()
    fetch_stats = pltpu.make_async_copy(stat_hbm, stats, sems.at[chunks + 1])
    fetch_stats.start()
    keep_ref[:owners] = jnp.zeros((owners,) + keep_ref.shape[1:], BF)
    send_ref[:owners] = jnp.zeros((owners,) + keep_ref.shape[1:], BF)
    fetch.wait()
    for chunk in range(chunks):
        copies[chunk].wait()

        def move(step, carry):
            block = chunk * size + step
            slot = slots[block]
            owner = slot // 2
            place = (owner % ny) * nz + owner // ny
            mine = slot % 2 == core
            tile = grads[block]
            keep_ref[jnp.where(mine, place, dump)] = tile
            send_ref[jnp.where(mine, dump, place)] = tile
            return carry

        lax.fori_loop(0, size, move, 0, unroll=8)
    fetch_stats.wait()
    tail_shape = (dump - owners,) + keep_ref.shape[1:]
    keep_ref[owners:dump] = stats[core].reshape(tail_shape).astype(BF)
    send_ref[owners:dump] = stats[1 - core].reshape(tail_shape).astype(BF)


def quarter_kernel(nx, keep_ref, got_ref, out_ref, stat_ref):
    owners = out_ref.shape[1] * out_ref.shape[2]
    width = out_ref.shape[-1]
    core = lax.axis_index("core")
    for part in range(nx):
        cols = slice(part * width, (part + 1) * width)
        total = keep_ref[:owners, :, cols].astype(F32) + got_ref[:owners, :, cols].astype(F32)
        out_ref[part] = total.astype(BF).reshape(out_ref.shape[1:])
    half = stat_ref.shape[1] // 2
    for ref, place in ((keep_ref, core), (got_ref, 1 - core)):
        rows = pl.ds(pl.multiple_of(place * half, half), half)
        stat_ref[:, rows, :] = ref[owners:-1].reshape(2, half, stat_ref.shape[2])


def sum_kernel(in_ref, out_ref):
    nx, ny = in_ref.shape[:2]
    for part in range(ny):
        total = in_ref[0, part].astype(F32)
        for copy in range(1, nx):
            total = total + in_ref[copy, part].astype(F32)
        out_ref[:, part] = total.astype(BF)


def fan_kernel(in_ref, stat_ref, out_ref):
    nx = out_ref.shape[0]
    order, width = in_ref.shape
    x = lax.axis_index("x")

    def columns(side, shift):
        return stat_ref[side, :, pl.ds(pl.multiple_of(lax.rem(x + shift, nx) * width, width), width)]

    for chip in range(nx):
        out_ref[chip, :order] = in_ref[...]
    for shift in range(1, nx):
        chip = lax.rem(x - shift + nx, nx)
        for side in range(2):
            base = order + 2 * side * width
            out_ref[chip, base : base + width] = columns(side, 0)
            out_ref[chip, base + width : base + 2 * width] = columns(side, 1 if shift < nx - 1 else 2)


def dot(left, right, contract=((1,), (0,))):
    return lax.dot_general(left, right, (contract, ((), ())), preferred_element_type=F32)


def step_kernel(own_ref, got_ref, out_ref, grad_ref, stat_ref):
    nx, _, width = got_ref.shape
    order = grad_ref.shape[0]
    x = lax.axis_index("x")
    for part in range(nx):
        grad_ref[:, part * width : (part + 1) * width] = got_ref[part, :order]

    eye = (
        lax.broadcasted_iota(jnp.int32, (width, width), 0) == lax.broadcasted_iota(jnp.int32, (width, width), 1)
    ).astype(BF)

    def at(shift):
        return pl.ds(pl.multiple_of(lax.rem(x + shift, nx) * width, width), width)

    for side in range(2):
        stat_ref[side, at(0), :] = own_ref[side]
        for shift in range(1, nx):
            block = own_ref[side, :, at(shift)]
            stat_ref[side, at(shift), at(0)] = dot(eye, block, ((1,), (1,))).astype(BF)
            source = lax.rem(x + shift, nx)
            partner = shift % (nx - 1) + 1
            base = order + 2 * side * width
            stat_ref[side, at(shift), at(shift)] = got_ref[source, base : base + width]
            block = got_ref[source, base + width : base + 2 * width]
            stat_ref[side, at(shift), at(partner)] = block
            stat_ref[side, at(partner), at(shift)] = dot(eye, block, ((1,), (1,))).astype(BF)

    grad = grad_ref[...]
    row_ids = lax.broadcasted_iota(jnp.int32, (order, order), 0)
    col_ids = lax.broadcasted_iota(jnp.int32, (order, order), 1)
    diagonal = row_ids == col_ids
    sides = range(2)
    grams = [dot(grad, grad, ((1,), (1,))), dot(grad, grad, ((0,), (0,)))]
    deltas = []
    for side in sides:
        shifted = decay_rate * stat_ref[side].astype(F32) + grams[side] + jnp.where(diagonal, ridge_term, 0.0)
        deltas.append(shifted * (-0.25 * start_scale * lax.rsqrt(jnp.sum(shifted * shifted))))
    lows = [delta.astype(BF) for delta in deltas]
    squares = [dot(low, low) for low in lows]
    seconds = [
        (squares[side] + 2.5 * deltas[side] + jnp.where(diagonal, 1.5625, 0.0)).astype(BF) for side in sides
    ]
    tails = [(1.25 * deltas[side] + squares[side]).astype(BF) for side in sides]
    fourths = [dot(second, second).astype(BF) for second in seconds]
    roots = [
        (dot(fourths[side], tails[side]) + 1.25 * deltas[side] + jnp.where(diagonal, 1.5625, 0.0)).astype(BF)
        for side in sides
    ]
    half = dot(roots[0], grad).astype(BF)
    precond = dot(half, roots[1])
    count = float(order * order)
    grad32 = grad.astype(F32)
    mean_grad = jnp.sum(grad32 * grad32) / count
    mean_pre = jnp.sum(precond * precond) / count
    scale = jnp.sqrt(mean_grad) / jnp.sqrt(mean_pre + graft_floor)
    for part in range(nx):

        @pl.when(x == part)
        def _():
            out_ref[...] = (precond[:, part * width : (part + 1) * width] * scale).astype(BF)


def spread_kernel(in_ref, out_ref):
    nx, ny = out_ref.shape[:2]
    for part in range(ny):
        piece = in_ref[:, part]
        for copy in range(nx):
            out_ref[copy, part] = piece


def pick_kernel(chunks, slot_ref, own_ref, got_ref, out_hbm, slots, out, sems):
    nx, ny, nz = own_ref.shape[:3]
    width = own_ref.shape[-1]
    blocks = out.shape[0]
    size = blocks // chunks
    core = lax.axis_index("core")
    fetch = pltpu.make_async_copy(slot_ref, slots, sems.at[chunks])
    fetch.start()
    fetch.wait()
    copies = []
    for chunk in range(chunks):

        def move(step, carry):
            block = chunk * size + step
            slot = slots[block]
            owner = slot // 2
            y, z = owner % ny, owner // ny
            mine = slot % 2 == core
            for part in range(nx):
                out[block, :, part * width : (part + 1) * width] = jnp.where(
                    mine, own_ref[part, y, z], got_ref[part, y, z]
                )
            return carry

        lax.fori_loop(0, size, move, 0, unroll=8)
        span = pl.ds(chunk * size, size)
        copies.append(pltpu.make_async_copy(out.at[span], out_hbm.at[span], sems.at[chunk]))
        copies[-1].start()
    for copy in copies:
        copy.wait()


def shaped(shape, dtype=BF):
    return jax.ShapeDtypeStruct(shape, dtype)


def on_device(gradients, old_stats, owner_slot):
    nx, nz, ny = lax.axis_size("x"), lax.axis_size("shard"), lax.axis_size("tensor")
    blocks, rows, order = gradients.shape[1:]
    owners = ny * nz
    width = order // nx
    stat_rows = old_stats.shape[2]
    tail = 2 * stat_rows // rows
    swap = [(0, 1), (1, 0)]
    exchange = functools.partial(lax.all_to_all, split_axis=0, concat_axis=0, tiled=True)

    whole = (owners + tail + 1, rows, order)
    chunks = 4
    keep, send = call(
        functools.partial(place_kernel, ny, nz, chunks),
        [shaped(whole), shaped(whole)],
        "hhh",
        scratch=[
            pltpu.SMEM(owner_slot.shape, jnp.int32),
            pltpu.VMEM((blocks, rows, order), BF),
            pltpu.VMEM(old_stats.shape, F32),
            pltpu.SemaphoreType.DMA((chunks + 2,)),
        ],
    )(*(pltpu.with_memory_space_constraint(array, pltpu.HBM) for array in (owner_slot, gradients, old_stats)))
    got = lax.ppermute(send, "core", swap)
    parts, stat = call(
        functools.partial(quarter_kernel, nx),
        [shaped((nx, ny, nz, rows, width)), shaped((2, 2 * stat_rows, order))],
        "vv",
    )(keep, got)
    parts = exchange(parts.reshape(nx * ny, nz, rows, width), ("x", "tensor"))
    summed = call(sum_kernel, shaped((nz, ny, rows, width)), "v")(parts.reshape(nx, ny, nz, rows, width))
    quarter_grad = exchange(summed, "shard").reshape(order, width)
    fanned = call(fan_kernel, shaped((nx, order + 4 * width, width)), "vv")(quarter_grad, stat)
    gathered = exchange(fanned, "x")
    update = call(
        step_kernel,
        shaped((order, width)),
        "vv",
        scratch=[pltpu.VMEM((order, order), BF), pltpu.VMEM((2, order, order), BF)],
        flops=20 * order**3,
        nbytes=2 << 20,
    )(stat, gathered)
    back = exchange(update.reshape(nz, ny, rows, width), "shard")
    spread = call(spread_kernel, shaped((nx, ny, nz, rows, width)), "v")(back)
    own = exchange(spread.reshape(nx * ny, nz, rows, width), ("x", "tensor"))
    own = own.reshape(nx, ny, nz, rows, width)
    return call(
        functools.partial(pick_kernel, chunks),
        shaped((blocks, rows, order)),
        "vvv",
        scratch=[
            pltpu.SMEM(owner_slot.shape, jnp.int32),
            pltpu.VMEM((blocks, rows, order), BF),
            pltpu.SemaphoreType.DMA((chunks + 1,)),
        ],
        out_kind="h",
    )(owner_slot, own, lax.ppermute(own, "core", swap))


def solution(mesh):
    replica, nz, ny = (mesh.shape[name] for name in ("replica", "shard", "tensor"))
    fine = Mesh(mesh.devices.reshape(replica // 2, 2, nz, ny), ("x", "core", "shard", "tensor"))
    replicas, rows = ("x", "core"), ("shard", "tensor")
    return jax.shard_map(
        on_device,
        mesh=fine,
        in_specs=(P(replicas, None, rows, None), P(rows, None, replicas, None), P()),
        out_specs=P(None, rows, None),
        check_vma=False,
    )
```

```python
import functools

import jax
import jax.numpy as jnp
from jax import lax
from jax.experimental import pallas as pl
from jax.experimental.pallas import tpu as pltpu
from jax.sharding import Mesh, PartitionSpec as P

ridge_term = 1e-06
decay_rate = 0.95
graft_floor = 1e-06
start_scale = 4.0

BF = jnp.bfloat16
F32 = jnp.float32
VMEM_LIMIT = 48 * 1024 * 1024


def call(kernel, out_shape, in_kinds, scratch=(), out_kind="v", flops=0, nbytes=1 << 20):
    kinds = {"v": pltpu.VMEM, "h": pltpu.HBM}
    single = not isinstance(out_shape, (list, tuple))
    spec = pl.BlockSpec(memory_space=kinds[out_kind])
    return pl.pallas_call(
        kernel,
        out_shape=out_shape,
        in_specs=[pl.BlockSpec(memory_space=kinds[k]) for k in in_kinds],
        out_specs=spec if single else [spec] * len(out_shape),
        scratch_shapes=list(scratch),
        compiler_params=pltpu.CompilerParams(vmem_limit_bytes=VMEM_LIMIT),
        cost_estimate=pl.CostEstimate(flops=flops, bytes_accessed=nbytes, transcendentals=0),
    )


def split(slot, ny):
    owner = slot >> 1
    return owner & (ny - 1), owner >> (ny.bit_length() - 1), slot & 1


def place_kernel(ny, nz, chunks, slot_hbm, grad_hbm, stat_hbm, keep_ref, send_ref, slots, grads, stats, sems):
    blocks = grads.shape[0]
    owners = ny * nz
    dump = keep_ref.shape[0] - 1
    size = blocks // chunks
    core = lax.axis_index("core")
    fetch = pltpu.make_async_copy(slot_hbm, slots, sems.at[chunks])
    fetch.start()
    copies = []
    for chunk in range(chunks):
        span = pl.ds(chunk * size, size)
        copies.append(pltpu.make_async_copy(grad_hbm.at[0, span], grads.at[span], sems.at[chunk]))
        copies[-1].start()
    fetch_stats = pltpu.make_async_copy(stat_hbm, stats, sems.at[chunks + 1])
    fetch_stats.start()
    keep_ref[:owners] = jnp.zeros((owners,) + keep_ref.shape[1:], BF)
    send_ref[:owners] = jnp.zeros((owners,) + keep_ref.shape[1:], BF)
    fetch.wait()
    for chunk in range(chunks):
        copies[chunk].wait()

        def move(step, carry):
            block = chunk * size + step
            y, z, part = split(slots[block], ny)
            place = y * nz + z
            mine = part == core
            tile = grads[block]
            keep_ref[jnp.where(mine, place, dump)] = tile
            send_ref[jnp.where(mine, dump, place)] = tile
            return carry

        lax.fori_loop(0, size, move, 0, unroll=8)
    fetch_stats.wait()
    tail_shape = (dump - owners,) + keep_ref.shape[1:]
    keep_ref[owners:dump] = stats[core].reshape(tail_shape).astype(BF)
    send_ref[owners:dump] = stats[1 - core].reshape(tail_shape).astype(BF)


def quarter_kernel(nx, keep_ref, got_ref, out_ref, stat_ref):
    owners = out_ref.shape[1] * out_ref.shape[2]
    width = out_ref.shape[-1]
    core = lax.axis_index("core")
    for part in range(nx):
        cols = slice(part * width, (part + 1) * width)
        total = keep_ref[:owners, :, cols].astype(F32) + got_ref[:owners, :, cols].astype(F32)
        out_ref[part] = total.astype(BF).reshape(out_ref.shape[1:])
    half = stat_ref.shape[1] // 2
    for ref, place in ((keep_ref, core), (got_ref, 1 - core)):
        rows = pl.ds(pl.multiple_of(place * half, half), half)
        stat_ref[:, rows, :] = ref[owners:-1].reshape(2, half, stat_ref.shape[2])


def sum_kernel(in_ref, out_ref):
    nx, ny = in_ref.shape[:2]
    for part in range(ny):
        total = in_ref[0, part].astype(F32)
        for copy in range(1, nx):
            total = total + in_ref[copy, part].astype(F32)
        out_ref[:, part] = total.astype(BF)


def fan_stats(stat_ref, out_ref, base):
    nx, _, width = out_ref.shape
    x = lax.axis_index("x")

    def columns(side, shift):
        return stat_ref[side, :, pl.ds(pl.multiple_of(lax.rem(x + shift, nx) * width, width), width)]

    for shift in range(1, nx):
        chip = lax.rem(x - shift + nx, nx)
        for side in range(2):
            start = base + 2 * side * width
            out_ref[chip, start : start + width] = columns(side, 0)
            out_ref[chip, start + width : start + 2 * width] = columns(side, 1 if shift < nx - 1 else 2)


def fan_stats_kernel(stat_ref, out_ref):
    fan_stats(stat_ref, out_ref, 0)


def fan_grad_kernel(in_ref, out_ref):
    for chip in range(out_ref.shape[0]):
        out_ref[chip] = in_ref[...]


def fan_both_kernel(in_ref, stat_ref, out_ref):
    order = in_ref.shape[0]
    for chip in range(out_ref.shape[0]):
        out_ref[chip, :order] = in_ref[...]
    fan_stats(stat_ref, out_ref, order)


def dot(left, right, contract=((1,), (0,))):
    return lax.dot_general(left, right, (contract, ((), ())), preferred_element_type=F32)


def step_kernel(
    first,
    own_ref,
    got_ref,
    got_stat_ref,
    out_ref,
    grad_ref,
    stat_ref,
    shift_ref,
    low_ref,
    second_ref,
    tail_ref,
    root_ref,
    pre_ref,
):
    nx, _, width = got_ref.shape
    order = grad_ref.shape[0]
    x = lax.axis_index("x")
    for part in range(nx):
        grad_ref[:, part * width : (part + 1) * width] = got_ref[part, :order]

    def at(shift):
        return pl.ds(pl.multiple_of(lax.rem(x + shift, nx) * width, width), width)

    for side in range(2):
        stat_ref[side, at(0), :] = own_ref[side]
        for shift in range(1, nx):
            block = own_ref[side, :, at(shift)]
            stat_ref[side, at(shift), at(0)] = block.T
            source = lax.rem(x + shift, nx)
            partner = shift % (nx - 1) + 1
            base = first + 2 * side * width
            stat_ref[side, at(shift), at(shift)] = got_stat_ref[source, base : base + width]
            block = got_stat_ref[source, base + width : base + 2 * width]
            stat_ref[side, at(shift), at(partner)] = block
            stat_ref[side, at(partner), at(shift)] = block.T

    diagonal = lax.broadcasted_iota(jnp.int32, (order, order), 0) == lax.broadcasted_iota(
        jnp.int32, (order, order), 1
    )

    def with_diagonal(value, amount):
        return value + jnp.where(diagonal, amount, 0.0)

    scales = []
    for side in range(2):
        gram = dot(grad_ref[...], grad_ref[...], ((1 - side,), (1 - side,)))
        shifted = with_diagonal(gram + decay_rate * stat_ref[side].astype(F32), ridge_term)
        shift_ref[side] = shifted
        scales.append(-0.25 * start_scale * lax.rsqrt(jnp.sum(shifted * shifted)))
    for side in range(2):
        low_ref[side] = (shift_ref[side] * scales[side]).astype(BF)
    for side in range(2):
        squared = dot(low_ref[side], low_ref[side])
        second_ref[side] = with_diagonal(squared + shift_ref[side] * (2.5 * scales[side]), 1.5625).astype(BF)
        tail_ref[side] = (squared + shift_ref[side] * (1.25 * scales[side])).astype(BF)

    def root(side):
        fourth = dot(second_ref[side], second_ref[side]).astype(BF)
        value = dot(fourth, tail_ref[side]) + shift_ref[side] * (1.25 * scales[side])
        return with_diagonal(value, 1.5625).astype(BF)

    root_ref[...] = root(1)
    half = dot(root(0), grad_ref[...]).astype(BF)
    precond = dot(half, root_ref[...])
    pre_ref[...] = precond
    grad32 = grad_ref[...].astype(F32)
    count = float(order * order)
    mean_grad = jnp.sum(grad32 * grad32) / count
    mean_pre = jnp.sum(precond * precond) / count
    scale = jnp.sqrt(mean_grad) / jnp.sqrt(mean_pre + graft_floor)
    out_ref[...] = (pre_ref[:, at(0)] * scale).astype(BF)


def spread_kernel(in_ref, out_ref):
    nx, ny = out_ref.shape[:2]
    for part in range(ny):
        piece = in_ref[:, part]
        for copy in range(nx):
            out_ref[copy, part] = piece


def pick_kernel(slot_ref, own_ref, got_ref, out_hbm, slots, out, sems):
    nx, ny = own_ref.shape[:2]
    width = own_ref.shape[-1]
    core = lax.axis_index("core")
    fetch = pltpu.make_async_copy(slot_ref, slots, sems.at[0])
    fetch.start()
    fetch.wait()

    def move(block, carry):
        y, z, place = split(slots[block], ny)
        mine = place == core
        for part in range(nx):
            out[block, :, part * width : (part + 1) * width] = jnp.where(
                mine, own_ref[part, y, z], got_ref[part, y, z]
            )
        return carry

    lax.fori_loop(0, out.shape[0], move, 0, unroll=8)
    store = pltpu.make_async_copy(out, out_hbm, sems.at[1])
    store.start()
    store.wait()


def shaped(shape, dtype=BF):
    return jax.ShapeDtypeStruct(shape, dtype)


def on_device(gradients, old_stats, owner_slot):
    nx, nz, ny = lax.axis_size("x"), lax.axis_size("shard"), lax.axis_size("tensor")
    blocks, rows, order = gradients.shape[1:]
    owners = ny * nz
    width = order // nx
    stat_rows = old_stats.shape[2]
    tail = 2 * stat_rows // rows
    swap = [(0, 1), (1, 0)]
    exchange = functools.partial(lax.all_to_all, split_axis=0, concat_axis=0, tiled=True)

    whole = (owners + tail + 1, rows, order)
    chunks = 2
    keep, send = call(
        functools.partial(place_kernel, ny, nz, chunks),
        [shaped(whole), shaped(whole)],
        "hhh",
        scratch=[
            pltpu.SMEM(owner_slot.shape, jnp.int32),
            pltpu.VMEM((blocks, rows, order), BF),
            pltpu.VMEM(old_stats.shape, F32),
            pltpu.SemaphoreType.DMA((chunks + 2,)),
        ],
    )(*(pltpu.with_memory_space_constraint(array, pltpu.HBM) for array in (owner_slot, gradients, old_stats)))
    got = lax.ppermute(send, "core", swap)
    parts, stat = call(
        functools.partial(quarter_kernel, nx),
        [shaped((nx, ny, nz, rows, width)), shaped((2, 2 * stat_rows, order))],
        "vv",
    )(keep, got)

    def quarter_of(pieces):
        pieces = exchange(pieces.reshape(nx * ny, nz, rows, width), ("x", "tensor")).reshape(pieces.shape)
        pieces = call(sum_kernel, shaped((nz, ny, rows, width)), "v")(pieces)
        return exchange(pieces, "shard").reshape(order, width)

    def step(first, *arrays):
        return call(
            functools.partial(step_kernel, first),
            shaped((order, width)),
            "vvv",
            scratch=[
                pltpu.VMEM((order, order), BF),
                pltpu.VMEM((2, order, order), BF),
                pltpu.VMEM((2, order, order), F32),
                pltpu.VMEM((2, order, order), BF),
                pltpu.VMEM((2, order, order), BF),
                pltpu.VMEM((2, order, order), BF),
                pltpu.VMEM((order, order), BF),
                pltpu.VMEM((order, order), F32),
            ],
            flops=20 * order**3,
            nbytes=2 << 20,
        )(*arrays)

    def stats_late(pieces, stat):
        whole_shape = shaped((nx, order + 4 * width, width))
        both = exchange(call(fan_both_kernel, whole_shape, "vv")(quarter_of(pieces), stat), "x")
        return step(order, stat, both, both)

    def stats_early(pieces, stat):
        got_stat = exchange(call(fan_stats_kernel, shaped((nx, 4 * width, width)), "v")(stat), "x")
        pieces, got_stat = lax.optimization_barrier((pieces, got_stat))
        quarters = call(fan_grad_kernel, shaped((nx, order, width)), "v")(quarter_of(pieces))
        return step(0, stat, exchange(quarters, "x"), got_stat)

    update = lax.cond(lax.axis_index("core") == 0, stats_late, stats_early, parts, stat)
    back = exchange(update.reshape(nz, ny, rows, width), "shard")
    spread = call(spread_kernel, shaped((nx, ny, nz, rows, width)), "v")(back)
    own = exchange(spread.reshape(nx * ny, nz, rows, width), ("x", "tensor"))
    own = own.reshape(nx, ny, nz, rows, width)
    return call(
        pick_kernel,
        shaped((blocks, rows, order)),
        "vvv",
        scratch=[
            pltpu.SMEM(owner_slot.shape, jnp.int32),
            pltpu.VMEM((blocks, rows, order), BF),
            pltpu.SemaphoreType.DMA((2,)),
        ],
        out_kind="h",
    )(owner_slot, own, lax.ppermute(own, "core", swap))


def solution(mesh):
    replica, nz, ny = (mesh.shape[name] for name in ("replica", "shard", "tensor"))
    fine = Mesh(mesh.devices.reshape(replica // 2, 2, nz, ny), ("x", "core", "shard", "tensor"))
    replicas, rows = ("x", "core"), ("shard", "tensor")
    return jax.shard_map(
        on_device,
        mesh=fine,
        in_specs=(P(replicas, None, rows, None), P(rows, None, replicas, None), P()),
        out_specs=P(None, rows, None),
        check_vma=False,
    )
```

```python
import functools

import jax
import jax.numpy as jnp
from jax import lax
from jax.experimental import pallas as pl
from jax.experimental.pallas import tpu as pltpu
from jax.sharding import Mesh, PartitionSpec as P

ridge_term = 1e-06
decay_rate = 0.95
graft_floor = 1e-06
start_scale = 4.0

BF = jnp.bfloat16
F32 = jnp.float32
VMEM_LIMIT = 48 * 1024 * 1024


def call(kernel, out_shape, in_kinds, scratch=(), out_kind="v", flops=0, nbytes=1 << 20):
    kinds = {"v": pltpu.VMEM, "h": pltpu.HBM}
    single = not isinstance(out_shape, (list, tuple))
    spec = pl.BlockSpec(memory_space=kinds[out_kind])
    return pl.pallas_call(
        kernel,
        out_shape=out_shape,
        in_specs=[pl.BlockSpec(memory_space=kinds[k]) for k in in_kinds],
        out_specs=spec if single else [spec] * len(out_shape),
        scratch_shapes=list(scratch),
        compiler_params=pltpu.CompilerParams(vmem_limit_bytes=VMEM_LIMIT),
        cost_estimate=pl.CostEstimate(flops=flops, bytes_accessed=nbytes, transcendentals=0),
    )


def split(slot, ny):
    owner = slot >> 1
    return owner & (ny - 1), owner >> (ny.bit_length() - 1), slot & 1


def place_kernel(ny, nz, chunks, slot_hbm, grad_hbm, stat_hbm, keep_ref, send_ref, slots, grads, stats, sems):
    blocks = grads.shape[0]
    owners = ny * nz
    dump = keep_ref.shape[0] - 1
    size = blocks // chunks
    core = lax.axis_index("core")
    fetch = pltpu.make_async_copy(slot_hbm, slots, sems.at[chunks])
    fetch.start()
    copies = []
    for chunk in range(chunks):
        span = pl.ds(chunk * size, size)
        copies.append(pltpu.make_async_copy(grad_hbm.at[0, span], grads.at[span], sems.at[chunk]))
        copies[-1].start()
    fetch_stats = pltpu.make_async_copy(stat_hbm, stats, sems.at[chunks + 1])
    fetch_stats.start()
    keep_ref[:owners] = jnp.zeros((owners,) + keep_ref.shape[1:], BF)
    send_ref[:owners] = jnp.zeros((owners,) + keep_ref.shape[1:], BF)
    fetch.wait()
    for chunk in range(chunks):
        copies[chunk].wait()

        def move(step, carry):
            block = chunk * size + step
            y, z, part = split(slots[block], ny)
            place = y * nz + z
            mine = part == core
            tile = grads[block]
            keep_ref[jnp.where(mine, place, dump)] = tile
            send_ref[jnp.where(mine, dump, place)] = tile
            return carry

        lax.fori_loop(0, size, move, 0, unroll=8)
    fetch_stats.wait()
    tail_shape = (dump - owners,) + keep_ref.shape[1:]
    keep_ref[owners:dump] = stats[core].reshape(tail_shape).astype(BF)
    send_ref[owners:dump] = stats[1 - core].reshape(tail_shape).astype(BF)


def quarter_kernel(nx, keep_ref, got_ref, out_ref, stat_ref):
    owners = out_ref.shape[1] * out_ref.shape[2]
    width = out_ref.shape[-1]
    core = lax.axis_index("core")
    for part in range(nx):
        cols = slice(part * width, (part + 1) * width)
        total = keep_ref[:owners, :, cols].astype(F32) + got_ref[:owners, :, cols].astype(F32)
        out_ref[part] = total.astype(BF).reshape(out_ref.shape[1:])
    half = stat_ref.shape[1] // 2
    for ref, place in ((keep_ref, core), (got_ref, 1 - core)):
        rows = pl.ds(pl.multiple_of(place * half, half), half)
        stat_ref[:, rows, :] = ref[owners:-1].reshape(2, half, stat_ref.shape[2])


def sum_kernel(in_ref, out_ref):
    nx, ny = in_ref.shape[:2]
    for part in range(ny):
        total = in_ref[0, part].astype(F32)
        for copy in range(1, nx):
            total = total + in_ref[copy, part].astype(F32)
        out_ref[:, part] = total.astype(BF)


def fan_stats(stat_ref, out_ref, base):
    nx, _, width = out_ref.shape
    x = lax.axis_index("x")

    def columns(side, shift):
        return stat_ref[side, :, pl.ds(pl.multiple_of(lax.rem(x + shift, nx) * width, width), width)]

    for shift in range(1, nx):
        chip = lax.rem(x - shift + nx, nx)
        for side in range(2):
            start = base + 2 * side * width
            out_ref[chip, start : start + width] = columns(side, 0)
            out_ref[chip, start + width : start + 2 * width] = columns(side, 1 if shift < nx - 1 else 2)


def fan_stats_kernel(stat_ref, out_ref):
    fan_stats(stat_ref, out_ref, 0)


def fan_grad_kernel(in_ref, out_ref):
    for chip in range(out_ref.shape[0]):
        out_ref[chip] = in_ref[...]


def fan_both_kernel(in_ref, stat_ref, out_ref):
    order = in_ref.shape[0]
    for chip in range(out_ref.shape[0]):
        out_ref[chip, :order] = in_ref[...]
    fan_stats(stat_ref, out_ref, order)


def dot(left, right, contract=((1,), (0,))):
    return lax.dot_general(left, right, (contract, ((), ())), preferred_element_type=F32)


def step_kernel(
    first,
    own_ref,
    got_ref,
    got_stat_ref,
    out_ref,
    grad_ref,
    stat_ref,
    shift_ref,
    low_ref,
    second_ref,
    tail_ref,
    root_ref,
    pre_ref,
):
    nx, _, width = got_ref.shape
    order = grad_ref.shape[0]
    x = lax.axis_index("x")
    for part in range(nx):
        grad_ref[:, part * width : (part + 1) * width] = got_ref[part, :order]

    def at(shift):
        return pl.ds(pl.multiple_of(lax.rem(x + shift, nx) * width, width), width)

    for side in range(2):
        stat_ref[side, at(0), :] = own_ref[side]
        for shift in range(1, nx):
            block = own_ref[side, :, at(shift)]
            stat_ref[side, at(shift), at(0)] = block.T
            source = lax.rem(x + shift, nx)
            partner = shift % (nx - 1) + 1
            base = first + 2 * side * width
            stat_ref[side, at(shift), at(shift)] = got_stat_ref[source, base : base + width]
            block = got_stat_ref[source, base + width : base + 2 * width]
            stat_ref[side, at(shift), at(partner)] = block
            stat_ref[side, at(partner), at(shift)] = block.T

    diagonal = lax.broadcasted_iota(jnp.int32, (order, order), 0) == lax.broadcasted_iota(
        jnp.int32, (order, order), 1
    )

    def with_diagonal(value, amount):
        return value + jnp.where(diagonal, amount, 0.0)

    scales = []
    for side in range(2):
        gram = dot(grad_ref[...], grad_ref[...], ((1 - side,), (1 - side,)))
        shifted = with_diagonal(gram + decay_rate * stat_ref[side].astype(F32), ridge_term)
        shift_ref[side] = shifted
        scales.append(-0.25 * start_scale * lax.rsqrt(jnp.sum(shifted * shifted)))
    for side in range(2):
        low_ref[side] = (shift_ref[side] * scales[side]).astype(BF)
    for side in range(2):
        squared = dot(low_ref[side], low_ref[side])
        second_ref[side] = with_diagonal(squared + shift_ref[side] * (2.5 * scales[side]), 1.5625).astype(BF)
        tail_ref[side] = (squared + shift_ref[side] * (1.25 * scales[side])).astype(BF)

    def root(side):
        fourth = dot(second_ref[side], second_ref[side]).astype(BF)
        value = dot(fourth, tail_ref[side]) + shift_ref[side] * (1.25 * scales[side])
        return with_diagonal(value, 1.5625).astype(BF)

    root_ref[...] = root(1)
    half = dot(root(0), grad_ref[...]).astype(BF)
    precond = dot(half, root_ref[...])
    pre_ref[...] = precond
    grad32 = grad_ref[...].astype(F32)
    count = float(order * order)
    mean_grad = jnp.sum(grad32 * grad32) / count
    mean_pre = jnp.sum(precond * precond) / count
    scale = jnp.sqrt(mean_grad) / jnp.sqrt(mean_pre + graft_floor)
    out_ref[...] = (pre_ref[:, at(0)] * scale).astype(BF)


def fan_swap_kernel(in_ref, out_ref):
    for part in range(in_ref.shape[1]):
        piece = in_ref[:, part]
        for chip in range(out_ref.shape[0]):
            out_ref[chip, part] = piece


def spread_kernel(in_ref, out_ref):
    nx, ny = out_ref.shape[:2]
    for part in range(ny):
        piece = in_ref[:, part]
        for copy in range(nx):
            out_ref[copy, part] = piece


def pick_kernel(slot_ref, own_ref, got_ref, out_hbm, slots, out, sems):
    nx, ny = own_ref.shape[:2]
    width = own_ref.shape[-1]
    core = lax.axis_index("core")
    fetch = pltpu.make_async_copy(slot_ref, slots, sems.at[0])
    fetch.start()
    fetch.wait()

    def move(block, carry):
        y, z, place = split(slots[block], ny)
        mine = place == core
        for part in range(nx):
            out[block, :, part * width : (part + 1) * width] = jnp.where(
                mine, own_ref[part, y, z], got_ref[part, y, z]
            )
        return carry

    size = out.shape[0] // 2
    stores = []
    for half in range(2):
        lax.fori_loop(half * size, (half + 1) * size, move, 0, unroll=8)
        span = pl.ds(half * size, size)
        stores.append(pltpu.make_async_copy(out.at[span], out_hbm.at[span], sems.at[1 + half]))
        stores[-1].start()
    for store in stores:
        store.wait()


def shaped(shape, dtype=BF):
    return jax.ShapeDtypeStruct(shape, dtype)


def on_device(gradients, old_stats, owner_slot):
    nx, nz, ny = lax.axis_size("x"), lax.axis_size("shard"), lax.axis_size("tensor")
    blocks, rows, order = gradients.shape[1:]
    owners = ny * nz
    width = order // nx
    stat_rows = old_stats.shape[2]
    tail = 2 * stat_rows // rows
    swap = [(0, 1), (1, 0)]
    exchange = functools.partial(lax.all_to_all, split_axis=0, concat_axis=0, tiled=True)

    whole = (owners + tail + 1, rows, order)
    chunks = 2
    keep, send = call(
        functools.partial(place_kernel, ny, nz, chunks),
        [shaped(whole), shaped(whole)],
        "hhh",
        scratch=[
            pltpu.SMEM(owner_slot.shape, jnp.int32),
            pltpu.VMEM((blocks, rows, order), BF),
            pltpu.VMEM(old_stats.shape, F32),
            pltpu.SemaphoreType.DMA((chunks + 2,)),
        ],
    )(*(pltpu.with_memory_space_constraint(array, pltpu.HBM) for array in (owner_slot, gradients, old_stats)))
    got = lax.ppermute(send, "core", swap)
    parts, stat = call(
        functools.partial(quarter_kernel, nx),
        [shaped((nx, ny, nz, rows, width)), shaped((2, 2 * stat_rows, order))],
        "vv",
    )(keep, got)

    def quarter_of(pieces):
        pieces = exchange(pieces.reshape(nx * ny, nz, rows, width), ("x", "tensor")).reshape(pieces.shape)
        pieces = call(sum_kernel, shaped((nz, ny, rows, width)), "v")(pieces)
        return exchange(pieces, "shard").reshape(order, width)

    def step(first, *arrays):
        return call(
            functools.partial(step_kernel, first),
            shaped((order, width)),
            "vvv",
            scratch=[
                pltpu.VMEM((order, order), BF),
                pltpu.VMEM((2, order, order), BF),
                pltpu.VMEM((2, order, order), F32),
                pltpu.VMEM((2, order, order), BF),
                pltpu.VMEM((2, order, order), BF),
                pltpu.VMEM((2, order, order), BF),
                pltpu.VMEM((order, order), BF),
                pltpu.VMEM((order, order), F32),
            ],
            flops=20 * order**3,
            nbytes=2 << 20,
        )(*arrays)

    def spread(update):
        back = exchange(update.reshape(nz, ny, rows, width), "shard")
        pieces = call(spread_kernel, shaped((nx, ny, nz, rows, width)), "v")(back)
        return exchange(pieces.reshape(nx * ny, nz, rows, width), ("x", "tensor")).reshape(pieces.shape)

    def stats_late(pieces, stat):
        whole_shape = shaped((nx, order + 4 * width, width))
        both = exchange(call(fan_both_kernel, whole_shape, "vv")(quarter_of(pieces), stat), "x")
        return spread(step(order, stat, both, both))

    def stats_early(pieces, stat):
        got_stat = exchange(call(fan_stats_kernel, shaped((nx, 4 * width, width)), "v")(stat), "x")
        pieces, got_stat = lax.optimization_barrier((pieces, got_stat))
        quarters = call(fan_grad_kernel, shaped((nx, order, width)), "v")(quarter_of(pieces))
        update = step(0, stat, exchange(quarters, "x"), got_stat)
        back = exchange(update.reshape(nz * ny, rows, width), ("shard", "tensor")).reshape(nz, ny, rows, width)
        back = call(fan_swap_kernel, shaped((nx, ny, nz, rows, width)), "v")(back)
        return exchange(back, "x")

    own = lax.cond(lax.axis_index("core") == 0, stats_late, stats_early, parts, stat)
    return call(
        pick_kernel,
        shaped((blocks, rows, order)),
        "vvv",
        scratch=[
            pltpu.SMEM(owner_slot.shape, jnp.int32),
            pltpu.VMEM((blocks, rows, order), BF),
            pltpu.SemaphoreType.DMA((3,)),
        ],
        out_kind="h",
    )(owner_slot, own, lax.ppermute(own, "core", swap))


def solution(mesh):
    replica, nz, ny = (mesh.shape[name] for name in ("replica", "shard", "tensor"))
    fine = Mesh(mesh.devices.reshape(replica // 2, 2, nz, ny), ("x", "core", "shard", "tensor"))
    replicas, rows = ("x", "core"), ("shard", "tensor")
    return jax.shard_map(
        on_device,
        mesh=fine,
        in_specs=(P(replicas, None, rows, None), P(rows, None, replicas, None), P()),
        out_specs=P(None, rows, None),
        check_vma=False,
    )
```

```python
import functools

import jax
import jax.numpy as jnp
from jax import lax
from jax.experimental import pallas as pl
from jax.experimental.pallas import tpu as pltpu
from jax.sharding import Mesh, PartitionSpec as P

ridge_term = 1e-06
decay_rate = 0.95
graft_floor = 1e-06
start_scale = 4.0

BF = jnp.bfloat16
F32 = jnp.float32
VMEM_LIMIT = 48 * 1024 * 1024


def call(kernel, out_shape, in_kinds, scratch=(), out_kind="v", flops=0, nbytes=1 << 20):
    kinds = {"v": pltpu.VMEM, "h": pltpu.HBM}
    single = not isinstance(out_shape, (list, tuple))
    spec = pl.BlockSpec(memory_space=kinds[out_kind])
    return pl.pallas_call(
        kernel,
        out_shape=out_shape,
        in_specs=[pl.BlockSpec(memory_space=kinds[k]) for k in in_kinds],
        out_specs=spec if single else [spec] * len(out_shape),
        scratch_shapes=list(scratch),
        compiler_params=pltpu.CompilerParams(vmem_limit_bytes=VMEM_LIMIT),
        cost_estimate=pl.CostEstimate(flops=flops, bytes_accessed=nbytes, transcendentals=0),
    )


def split(slot, ny):
    owner = slot >> 1
    return owner & (ny - 1), owner >> (ny.bit_length() - 1), slot & 1


def place_kernel(ny, nz, chunks, slot_hbm, grad_hbm, stat_hbm, keep_ref, send_ref, slots, grads, stats, sems):
    blocks = grads.shape[0]
    owners = ny * nz
    dump = keep_ref.shape[0] - 1
    size = blocks // chunks
    core = lax.axis_index("core")
    fetch = pltpu.make_async_copy(slot_hbm, slots, sems.at[chunks])
    fetch.start()
    copies = []
    for chunk in range(chunks):
        span = pl.ds(chunk * size, size)
        copies.append(pltpu.make_async_copy(grad_hbm.at[0, span], grads.at[span], sems.at[chunk]))
        copies[-1].start()
    fetch_stats = pltpu.make_async_copy(stat_hbm, stats, sems.at[chunks + 1])
    fetch_stats.start()
    keep_ref[:owners] = jnp.zeros((owners,) + keep_ref.shape[1:], BF)
    send_ref[:owners] = jnp.zeros((owners,) + keep_ref.shape[1:], BF)
    fetch.wait()
    for chunk in range(chunks):
        copies[chunk].wait()

        def move(step, carry):
            block = chunk * size + step
            y, z, part = split(slots[block], ny)
            place = y * nz + z
            mine = part == core
            tile = grads[block]
            keep_ref[jnp.where(mine, place, dump)] = tile
            send_ref[jnp.where(mine, dump, place)] = tile
            return carry

        lax.fori_loop(0, size, move, 0, unroll=8)
    fetch_stats.wait()
    tail_shape = (dump - owners,) + keep_ref.shape[1:]
    keep_ref[owners:dump] = stats[core].reshape(tail_shape).astype(BF)
    send_ref[owners:dump] = stats[1 - core].reshape(tail_shape).astype(BF)


def quarter_kernel(nx, keep_ref, got_ref, out_ref, stat_ref):
    owners = out_ref.shape[1] * out_ref.shape[2]
    width = out_ref.shape[-1]
    core = lax.axis_index("core")
    for part in range(nx):
        cols = slice(part * width, (part + 1) * width)
        total = keep_ref[:owners, :, cols].astype(F32) + got_ref[:owners, :, cols].astype(F32)
        out_ref[part] = total.astype(BF).reshape(out_ref.shape[1:])
    half = stat_ref.shape[1] // 2
    for ref, place in ((keep_ref, core), (got_ref, 1 - core)):
        rows = pl.ds(pl.multiple_of(place * half, half), half)
        stat_ref[:, rows, :] = ref[owners:-1].reshape(2, half, stat_ref.shape[2])


def sum_kernel(in_ref, out_ref):
    nx, ny = in_ref.shape[:2]
    for part in range(ny):
        total = in_ref[0, part].astype(F32)
        for copy in range(1, nx):
            total = total + in_ref[copy, part].astype(F32)
        out_ref[:, part] = total.astype(BF)


def fan_stats(stat_ref, out_ref, base):
    nx, _, width = out_ref.shape
    x = lax.axis_index("x")

    def columns(side, shift):
        return stat_ref[side, :, pl.ds(pl.multiple_of(lax.rem(x + shift, nx) * width, width), width)]

    for shift in range(1, nx):
        chip = lax.rem(x - shift + nx, nx)
        for side in range(2):
            start = base + 2 * side * width
            out_ref[chip, start : start + width] = columns(side, 0)
            out_ref[chip, start + width : start + 2 * width] = columns(side, 1 if shift < nx - 1 else 2)


def triangle(width):
    row_ids = lax.broadcasted_iota(jnp.int32, (width, width), 0)
    col_ids = lax.broadcasted_iota(jnp.int32, (width, width), 1)
    return row_ids > col_ids, row_ids == col_ids


def fan_packed_kernel(stat_ref, out_ref):
    nx, rows, width = out_ref.shape
    x = lax.axis_index("x")
    below, on = triangle(width)

    def columns(side, shift):
        return stat_ref[side, :, pl.ds(pl.multiple_of(lax.rem(x + shift, nx) * width, width), width)]

    left, right = columns(0, 0).astype(F32), columns(1, 0).astype(F32)
    mixed = jnp.where(below, right, left).astype(BF)
    line = jnp.sum(jnp.where(on, right, 0.0), axis=0, keepdims=True)
    line = jnp.broadcast_to(line, (rows - 3 * width, width)).astype(BF)
    for shift in range(1, nx):
        chip = lax.rem(x - shift + nx, nx)
        for side in range(2):
            out_ref[chip, side * width : (side + 1) * width] = columns(side, 1 if shift < nx - 1 else 2)
        out_ref[chip, 2 * width : 3 * width] = mixed
        out_ref[chip, 3 * width :] = line


def fan_grad_kernel(in_ref, out_ref):
    for chip in range(out_ref.shape[0]):
        out_ref[chip] = in_ref[...]


def fan_both_kernel(in_ref, stat_ref, out_ref):
    order = in_ref.shape[0]
    for chip in range(out_ref.shape[0]):
        out_ref[chip, :order] = in_ref[...]
    fan_stats(stat_ref, out_ref, order)


def dot(left, right, contract=((1,), (0,))):
    return lax.dot_general(left, right, (contract, ((), ())), preferred_element_type=F32)


def step_kernel(
    first,
    own_ref,
    got_ref,
    got_stat_ref,
    out_ref,
    grad_ref,
    stat_ref,
    shift_ref,
    low_ref,
    second_ref,
    tail_ref,
    root_ref,
    pre_ref,
):
    nx, _, width = got_ref.shape
    order = grad_ref.shape[0]
    x = lax.axis_index("x")
    for part in range(nx):
        grad_ref[:, part * width : (part + 1) * width] = got_ref[part, :order]

    def at(shift):
        return pl.ds(pl.multiple_of(lax.rem(x + shift, nx) * width, width), width)

    for side in range(2):
        stat_ref[side, at(0), :] = own_ref[side]
        for shift in range(1, nx):
            block = own_ref[side, :, at(shift)]
            stat_ref[side, at(shift), at(0)] = block.T
            source = lax.rem(x + shift, nx)
            partner = shift % (nx - 1) + 1
            if first:
                base = first + 2 * side * width
                own_block = got_stat_ref[source, base : base + width]
                block = got_stat_ref[source, base + width : base + 2 * width]
            else:
                below, on = triangle(width)
                mixed = got_stat_ref[source, 2 * width : 3 * width].astype(F32)
                line = got_stat_ref[source, 3 * width :].astype(F32)[:1]
                turned = mixed.T
                if side == 0:
                    own_block = jnp.where(below, turned, mixed).astype(BF)
                else:
                    own_block = jnp.where(below, mixed, jnp.where(on, line, turned)).astype(BF)
                block = got_stat_ref[source, side * width : (side + 1) * width]
            stat_ref[side, at(shift), at(shift)] = own_block
            stat_ref[side, at(shift), at(partner)] = block
            stat_ref[side, at(partner), at(shift)] = block.T

    diagonal = lax.broadcasted_iota(jnp.int32, (order, order), 0) == lax.broadcasted_iota(
        jnp.int32, (order, order), 1
    )

    def with_diagonal(value, amount):
        return value + jnp.where(diagonal, amount, 0.0)

    scales = []
    for side in range(2):
        gram = dot(grad_ref[...], grad_ref[...], ((1 - side,), (1 - side,)))
        shifted = with_diagonal(gram + decay_rate * stat_ref[side].astype(F32), ridge_term)
        shift_ref[side] = shifted
        scales.append(-0.25 * start_scale * lax.rsqrt(jnp.sum(shifted * shifted)))
    for side in range(2):
        low_ref[side] = (shift_ref[side] * scales[side]).astype(BF)
    for side in range(2):
        squared = dot(low_ref[side], low_ref[side])
        second_ref[side] = with_diagonal(squared + shift_ref[side] * (2.5 * scales[side]), 1.5625).astype(BF)
        tail_ref[side] = (squared + shift_ref[side] * (1.25 * scales[side])).astype(BF)

    def root(side):
        fourth = dot(second_ref[side], second_ref[side]).astype(BF)
        value = dot(fourth, tail_ref[side]) + shift_ref[side] * (1.25 * scales[side])
        return with_diagonal(value, 1.5625).astype(BF)

    root_ref[...] = root(1)
    half = dot(root(0), grad_ref[...]).astype(BF)
    precond = dot(half, root_ref[...])
    pre_ref[...] = precond
    grad32 = grad_ref[...].astype(F32)
    count = float(order * order)
    mean_grad = jnp.sum(grad32 * grad32) / count
    mean_pre = jnp.sum(precond * precond) / count
    scale = jnp.sqrt(mean_grad) / jnp.sqrt(mean_pre + graft_floor)
    out_ref[...] = (pre_ref[:, at(0)] * scale).astype(BF)


def fan_swap_kernel(in_ref, out_ref):
    for part in range(in_ref.shape[1]):
        piece = in_ref[:, part]
        for chip in range(out_ref.shape[0]):
            out_ref[chip, part] = piece


def spread_kernel(in_ref, out_ref):
    nx, ny = out_ref.shape[:2]
    for part in range(ny):
        piece = in_ref[:, part]
        for copy in range(nx):
            out_ref[copy, part] = piece


def pick_kernel(slot_ref, own_ref, got_ref, out_hbm, slots, out, sems):
    nx, ny = own_ref.shape[:2]
    width = own_ref.shape[-1]
    core = lax.axis_index("core")
    fetch = pltpu.make_async_copy(slot_ref, slots, sems.at[0])
    fetch.start()
    fetch.wait()

    def move(block, carry):
        y, z, place = split(slots[block], ny)
        mine = place == core
        for part in range(nx):
            out[block, :, part * width : (part + 1) * width] = jnp.where(
                mine, own_ref[part, y, z], got_ref[part, y, z]
            )
        return carry

    size = out.shape[0] // 2
    stores = []
    for half in range(2):
        lax.fori_loop(half * size, (half + 1) * size, move, 0, unroll=8)
        span = pl.ds(half * size, size)
        stores.append(pltpu.make_async_copy(out.at[span], out_hbm.at[span], sems.at[1 + half]))
        stores[-1].start()
    for store in stores:
        store.wait()


def shaped(shape, dtype=BF):
    return jax.ShapeDtypeStruct(shape, dtype)


def on_device(gradients, old_stats, owner_slot):
    nx, nz, ny = lax.axis_size("x"), lax.axis_size("shard"), lax.axis_size("tensor")
    blocks, rows, order = gradients.shape[1:]
    owners = ny * nz
    width = order // nx
    stat_rows = old_stats.shape[2]
    tail = 2 * stat_rows // rows
    swap = [(0, 1), (1, 0)]
    exchange = functools.partial(lax.all_to_all, split_axis=0, concat_axis=0, tiled=True)

    whole = (owners + tail + 1, rows, order)
    chunks = 2
    keep, send = call(
        functools.partial(place_kernel, ny, nz, chunks),
        [shaped(whole), shaped(whole)],
        "hhh",
        scratch=[
            pltpu.SMEM(owner_slot.shape, jnp.int32),
            pltpu.VMEM((blocks, rows, order), BF),
            pltpu.VMEM(old_stats.shape, F32),
            pltpu.SemaphoreType.DMA((chunks + 2,)),
        ],
    )(*(pltpu.with_memory_space_constraint(array, pltpu.HBM) for array in (owner_slot, gradients, old_stats)))
    got = lax.ppermute(send, "core", swap)
    parts, stat = call(
        functools.partial(quarter_kernel, nx),
        [shaped((nx, ny, nz, rows, width)), shaped((2, 2 * stat_rows, order))],
        "vv",
    )(keep, got)

    def quarter_of(pieces):
        pieces = exchange(pieces.reshape(nx * ny, nz, rows, width), ("x", "tensor")).reshape(pieces.shape)
        pieces = call(sum_kernel, shaped((nz, ny, rows, width)), "v")(pieces)
        return exchange(pieces, "shard").reshape(order, width)

    def step(first, *arrays):
        return call(
            functools.partial(step_kernel, first),
            shaped((order, width)),
            "vvv",
            scratch=[
                pltpu.VMEM((order, order), BF),
                pltpu.VMEM((2, order, order), BF),
                pltpu.VMEM((2, order, order), F32),
                pltpu.VMEM((2, order, order), BF),
                pltpu.VMEM((2, order, order), BF),
                pltpu.VMEM((2, order, order), BF),
                pltpu.VMEM((order, order), BF),
                pltpu.VMEM((order, order), F32),
            ],
            flops=20 * order**3,
            nbytes=2 << 20,
        )(*arrays)

    def spread(update):
        back = exchange(update.reshape(nz, ny, rows, width), "shard")
        pieces = call(spread_kernel, shaped((nx, ny, nz, rows, width)), "v")(back)
        return exchange(pieces.reshape(nx * ny, nz, rows, width), ("x", "tensor")).reshape(pieces.shape)

    def stats_late(pieces, stat):
        whole_shape = shaped((nx, order + 4 * width, width))
        both = exchange(call(fan_both_kernel, whole_shape, "vv")(quarter_of(pieces), stat), "x")
        return spread(step(order, stat, both, both))

    def stats_early(pieces, stat):
        got_stat = exchange(call(fan_packed_kernel, shaped((nx, 3 * width + 16, width)), "v")(stat), "x")
        pieces, got_stat = lax.optimization_barrier((pieces, got_stat))
        quarters = call(fan_grad_kernel, shaped((nx, order, width)), "v")(quarter_of(pieces))
        update = step(0, stat, exchange(quarters, "x"), got_stat)
        back = exchange(update.reshape(nz * ny, rows, width), ("shard", "tensor")).reshape(nz, ny, rows, width)
        back = call(fan_swap_kernel, shaped((nx, ny, nz, rows, width)), "v")(back)
        return exchange(back, "x")

    own = lax.cond(lax.axis_index("core") == 0, stats_late, stats_early, parts, stat)
    return call(
        pick_kernel,
        shaped((blocks, rows, order)),
        "vvv",
        scratch=[
            pltpu.SMEM(owner_slot.shape, jnp.int32),
            pltpu.VMEM((blocks, rows, order), BF),
            pltpu.SemaphoreType.DMA((3,)),
        ],
        out_kind="h",
    )(owner_slot, own, lax.ppermute(own, "core", swap))


def solution(mesh):
    replica, nz, ny = (mesh.shape[name] for name in ("replica", "shard", "tensor"))
    fine = Mesh(mesh.devices.reshape(replica // 2, 2, nz, ny), ("x", "core", "shard", "tensor"))
    replicas, rows = ("x", "core"), ("shard", "tensor")
    return jax.shard_map(
        on_device,
        mesh=fine,
        in_specs=(P(replicas, None, rows, None), P(rows, None, replicas, None), P()),
        out_specs=P(None, rows, None),
        check_vma=False,
    )
```

```python
import functools

import jax
import jax.numpy as jnp
from jax import lax
from jax.experimental import pallas as pl
from jax.experimental.pallas import tpu as pltpu
from jax.sharding import Mesh, PartitionSpec as P

ridge_term = 1e-06
decay_rate = 0.95
graft_floor = 1e-06
start_scale = 4.0

BF = jnp.bfloat16
F32 = jnp.float32
VMEM_LIMIT = 48 * 1024 * 1024


def call(kernel, out_shape, in_kinds, scratch=(), out_kind="v", flops=0, nbytes=1 << 20):
    kinds = {"v": pltpu.VMEM, "h": pltpu.HBM}
    single = not isinstance(out_shape, (list, tuple))
    spec = pl.BlockSpec(memory_space=kinds[out_kind])
    return pl.pallas_call(
        kernel,
        out_shape=out_shape,
        in_specs=[pl.BlockSpec(memory_space=kinds[k]) for k in in_kinds],
        out_specs=spec if single else [spec] * len(out_shape),
        scratch_shapes=list(scratch),
        compiler_params=pltpu.CompilerParams(vmem_limit_bytes=VMEM_LIMIT),
        cost_estimate=pl.CostEstimate(flops=flops, bytes_accessed=nbytes, transcendentals=0),
    )


def split(slot, ny):
    owner = slot >> 1
    return owner & (ny - 1), owner >> (ny.bit_length() - 1), slot & 1


def place_kernel(ny, nz, chunks, slot_hbm, grad_hbm, stat_hbm, keep_ref, send_ref, slots, grads, stats, sems):
    blocks = grads.shape[0]
    owners = ny * nz
    dump = keep_ref.shape[0] - 1
    size = blocks // chunks
    core = lax.axis_index("core")
    fetch = pltpu.make_async_copy(slot_hbm, slots, sems.at[chunks])
    fetch.start()
    copies = []
    for chunk in range(chunks):
        span = pl.ds(chunk * size, size)
        copies.append(pltpu.make_async_copy(grad_hbm.at[0, span], grads.at[span], sems.at[chunk]))
        copies[-1].start()
    fetch_stats = pltpu.make_async_copy(stat_hbm, stats, sems.at[chunks + 1])
    fetch_stats.start()
    keep_ref[:owners] = jnp.zeros((owners,) + keep_ref.shape[1:], BF)
    send_ref[:owners] = jnp.zeros((owners,) + keep_ref.shape[1:], BF)
    fetch.wait()
    for chunk in range(chunks):
        copies[chunk].wait()

        def move(step, carry):
            block = chunk * size + step
            y, z, part = split(slots[block], ny)
            place = y * nz + z
            mine = part == core
            tile = grads[block]
            keep_ref[jnp.where(mine, place, dump)] = tile
            send_ref[jnp.where(mine, dump, place)] = tile
            return carry

        lax.fori_loop(0, size, move, 0, unroll=8)
    fetch_stats.wait()
    tail_shape = (dump - owners,) + keep_ref.shape[1:]
    keep_ref[owners:dump] = stats[core].reshape(tail_shape).astype(BF)
    send_ref[owners:dump] = stats[1 - core].reshape(tail_shape).astype(BF)


def quarter_kernel(nx, keep_ref, got_ref, out_ref, stat_ref):
    owners = out_ref.shape[1] * out_ref.shape[2]
    width = out_ref.shape[-1]
    core = lax.axis_index("core")
    for part in range(nx):
        cols = slice(part * width, (part + 1) * width)
        total = keep_ref[:owners, :, cols].astype(F32) + got_ref[:owners, :, cols].astype(F32)
        out_ref[part] = total.astype(BF).reshape(out_ref.shape[1:])
    half = stat_ref.shape[1] // 2
    for ref, place in ((keep_ref, core), (got_ref, 1 - core)):
        rows = pl.ds(pl.multiple_of(place * half, half), half)
        stat_ref[:, rows, :] = ref[owners:-1].reshape(2, half, stat_ref.shape[2])


def sum_kernel(in_ref, out_ref):
    nx, ny = in_ref.shape[:2]
    for part in range(ny):
        total = in_ref[0, part].astype(F32)
        for copy in range(1, nx):
            total = total + in_ref[copy, part].astype(F32)
        out_ref[:, part] = total.astype(BF)


def triangle(width):
    row_ids = lax.broadcasted_iota(jnp.int32, (width, width), 0)
    col_ids = lax.broadcasted_iota(jnp.int32, (width, width), 1)
    return row_ids > col_ids, row_ids == col_ids


def fan_packed(stat_ref, out_ref, base):
    nx, rows, width = out_ref.shape
    x = lax.axis_index("x")
    below, on = triangle(width)

    def columns(side, shift):
        return stat_ref[side, :, pl.ds(pl.multiple_of(lax.rem(x + shift, nx) * width, width), width)]

    left, right = columns(0, 0).astype(F32), columns(1, 0).astype(F32)
    mixed = jnp.where(below, right, left).astype(BF)
    line = jnp.sum(jnp.where(on, right, 0.0), axis=0, keepdims=True)
    line = jnp.broadcast_to(line, (rows - base - 3 * width, width)).astype(BF)
    for shift in range(1, nx):
        chip = lax.rem(x - shift + nx, nx)
        for side in range(2):
            out_ref[chip, base + side * width : base + (side + 1) * width] = columns(side, 1 if shift < nx - 1 else 2)
        out_ref[chip, base + 2 * width : base + 3 * width] = mixed
        out_ref[chip, base + 3 * width :] = line


def fan_packed_kernel(stat_ref, out_ref):
    fan_packed(stat_ref, out_ref, 0)


def fan_grad_kernel(in_ref, out_ref):
    for chip in range(out_ref.shape[0]):
        out_ref[chip] = in_ref[...]


def fan_both_kernel(in_ref, stat_ref, out_ref):
    order = in_ref.shape[0]
    for chip in range(out_ref.shape[0]):
        out_ref[chip, :order] = in_ref[...]
    fan_packed(stat_ref, out_ref, order)


def dot(left, right, contract=((1,), (0,))):
    return lax.dot_general(left, right, (contract, ((), ())), preferred_element_type=F32)


def step_kernel(
    first,
    own_ref,
    got_ref,
    got_stat_ref,
    out_ref,
    grad_ref,
    stat_ref,
    shift_ref,
    low_ref,
    second_ref,
    tail_ref,
    root_ref,
    pre_ref,
):
    nx, _, width = got_ref.shape
    order = grad_ref.shape[0]
    x = lax.axis_index("x")
    for part in range(nx):
        grad_ref[:, part * width : (part + 1) * width] = got_ref[part, :order]

    def at(shift):
        return pl.ds(pl.multiple_of(lax.rem(x + shift, nx) * width, width), width)

    for side in range(2):
        stat_ref[side, at(0), :] = own_ref[side]
        for shift in range(1, nx):
            block = own_ref[side, :, at(shift)]
            stat_ref[side, at(shift), at(0)] = block.T
            source = lax.rem(x + shift, nx)
            partner = shift % (nx - 1) + 1
            below, on = triangle(width)
            start = first + 2 * width
            mixed = got_stat_ref[source, start : start + width].astype(F32)
            line = got_stat_ref[source, start + width :].astype(F32)[:1]
            turned = mixed.T
            if side == 0:
                own_block = jnp.where(below, turned, mixed).astype(BF)
            else:
                own_block = jnp.where(below, mixed, jnp.where(on, line, turned)).astype(BF)
            start = first + side * width
            block = got_stat_ref[source, start : start + width]
            stat_ref[side, at(shift), at(shift)] = own_block
            stat_ref[side, at(shift), at(partner)] = block
            stat_ref[side, at(partner), at(shift)] = block.T

    diagonal = lax.broadcasted_iota(jnp.int32, (order, order), 0) == lax.broadcasted_iota(
        jnp.int32, (order, order), 1
    )

    def with_diagonal(value, amount):
        return value + jnp.where(diagonal, amount, 0.0)

    scales = []
    for side in range(2):
        gram = dot(grad_ref[...], grad_ref[...], ((1 - side,), (1 - side,)))
        shifted = with_diagonal(gram + decay_rate * stat_ref[side].astype(F32), ridge_term)
        shift_ref[side] = shifted
        scales.append(-0.25 * start_scale * lax.rsqrt(jnp.sum(shifted * shifted)))
    for side in range(2):
        low_ref[side] = (shift_ref[side] * scales[side]).astype(BF)
    for side in range(2):
        squared = dot(low_ref[side], low_ref[side])
        second_ref[side] = with_diagonal(squared + shift_ref[side] * (2.5 * scales[side]), 1.5625).astype(BF)
        tail_ref[side] = (squared + shift_ref[side] * (1.25 * scales[side])).astype(BF)

    def root(side):
        fourth = dot(second_ref[side], second_ref[side]).astype(BF)
        value = dot(fourth, tail_ref[side]) + shift_ref[side] * (1.25 * scales[side])
        return with_diagonal(value, 1.5625).astype(BF)

    root_ref[...] = root(1)
    half = dot(root(0), grad_ref[...]).astype(BF)
    precond = dot(half, root_ref[...])
    pre_ref[...] = precond
    grad32 = grad_ref[...].astype(F32)
    count = float(order * order)
    mean_grad = jnp.sum(grad32 * grad32) / count
    mean_pre = jnp.sum(precond * precond) / count
    scale = jnp.sqrt(mean_grad) / jnp.sqrt(mean_pre + graft_floor)
    out_ref[...] = (pre_ref[:, at(0)] * scale).astype(BF)


def fan_swap_kernel(in_ref, out_ref):
    for part in range(in_ref.shape[1]):
        piece = in_ref[:, part]
        for chip in range(out_ref.shape[0]):
            out_ref[chip, part] = piece


def spread_kernel(in_ref, out_ref):
    nx, ny = out_ref.shape[:2]
    for part in range(ny):
        piece = in_ref[:, part]
        for copy in range(nx):
            out_ref[copy, part] = piece


def pick_kernel(slot_ref, own_ref, got_ref, out_hbm, slots, out, sems):
    nx, ny = own_ref.shape[:2]
    width = own_ref.shape[-1]
    core = lax.axis_index("core")
    fetch = pltpu.make_async_copy(slot_ref, slots, sems.at[0])
    fetch.start()
    fetch.wait()

    def move(block, carry):
        y, z, place = split(slots[block], ny)
        mine = place == core
        for part in range(nx):
            out[block, :, part * width : (part + 1) * width] = jnp.where(
                mine, own_ref[part, y, z], got_ref[part, y, z]
            )
        return carry

    size = out.shape[0] // 2
    stores = []
    for half in range(2):
        lax.fori_loop(half * size, (half + 1) * size, move, 0, unroll=8)
        span = pl.ds(half * size, size)
        stores.append(pltpu.make_async_copy(out.at[span], out_hbm.at[span], sems.at[1 + half]))
        stores[-1].start()
    for store in stores:
        store.wait()


def shaped(shape, dtype=BF):
    return jax.ShapeDtypeStruct(shape, dtype)


def on_device(gradients, old_stats, owner_slot):
    nx, nz, ny = lax.axis_size("x"), lax.axis_size("shard"), lax.axis_size("tensor")
    blocks, rows, order = gradients.shape[1:]
    owners = ny * nz
    width = order // nx
    stat_rows = old_stats.shape[2]
    tail = 2 * stat_rows // rows
    swap = [(0, 1), (1, 0)]
    exchange = functools.partial(lax.all_to_all, split_axis=0, concat_axis=0, tiled=True)

    whole = (owners + tail + 1, rows, order)
    chunks = 2
    keep, send = call(
        functools.partial(place_kernel, ny, nz, chunks),
        [shaped(whole), shaped(whole)],
        "hhh",
        scratch=[
            pltpu.SMEM(owner_slot.shape, jnp.int32),
            pltpu.VMEM((blocks, rows, order), BF),
            pltpu.VMEM(old_stats.shape, F32),
            pltpu.SemaphoreType.DMA((chunks + 2,)),
        ],
    )(*(pltpu.with_memory_space_constraint(array, pltpu.HBM) for array in (owner_slot, gradients, old_stats)))
    got = lax.ppermute(send, "core", swap)
    parts, stat = call(
        functools.partial(quarter_kernel, nx),
        [shaped((nx, ny, nz, rows, width)), shaped((2, 2 * stat_rows, order))],
        "vv",
    )(keep, got)

    def quarter_of(pieces):
        pieces = exchange(pieces.reshape(nx * ny, nz, rows, width), ("x", "tensor")).reshape(pieces.shape)
        pieces = call(sum_kernel, shaped((nz, ny, rows, width)), "v")(pieces)
        return exchange(pieces, "shard").reshape(order, width)

    def step(first, *arrays):
        return call(
            functools.partial(step_kernel, first),
            shaped((order, width)),
            "vvv",
            scratch=[
                pltpu.VMEM((order, order), BF),
                pltpu.VMEM((2, order, order), BF),
                pltpu.VMEM((2, order, order), F32),
                pltpu.VMEM((2, order, order), BF),
                pltpu.VMEM((2, order, order), BF),
                pltpu.VMEM((2, order, order), BF),
                pltpu.VMEM((order, order), BF),
                pltpu.VMEM((order, order), F32),
            ],
            flops=20 * order**3,
            nbytes=2 << 20,
        )(*arrays)

    def spread(update):
        back = exchange(update.reshape(nz, ny, rows, width), "shard")
        pieces = call(spread_kernel, shaped((nx, ny, nz, rows, width)), "v")(back)
        return exchange(pieces.reshape(nx * ny, nz, rows, width), ("x", "tensor")).reshape(pieces.shape)

    def stats_late(pieces, stat):
        whole_shape = shaped((nx, order + 3 * width + 16, width))
        both = exchange(call(fan_both_kernel, whole_shape, "vv")(quarter_of(pieces), stat), "x")
        return spread(step(order, stat, both, both))

    def stats_early(pieces, stat):
        got_stat = exchange(call(fan_packed_kernel, shaped((nx, 3 * width + 16, width)), "v")(stat), "x")
        pieces, got_stat = lax.optimization_barrier((pieces, got_stat))
        quarters = call(fan_grad_kernel, shaped((nx, order, width)), "v")(quarter_of(pieces))
        update = step(0, stat, exchange(quarters, "x"), got_stat)
        back = exchange(update.reshape(nz * ny, rows, width), ("shard", "tensor")).reshape(nz, ny, rows, width)
        back = call(fan_swap_kernel, shaped((nx, ny, nz, rows, width)), "v")(back)
        return exchange(back, "x")

    own = lax.cond(lax.axis_index("core") == 0, stats_late, stats_early, parts, stat)
    return call(
        pick_kernel,
        shaped((blocks, rows, order)),
        "vvv",
        scratch=[
            pltpu.SMEM(owner_slot.shape, jnp.int32),
            pltpu.VMEM((blocks, rows, order), BF),
            pltpu.SemaphoreType.DMA((3,)),
        ],
        out_kind="h",
    )(owner_slot, own, lax.ppermute(own, "core", swap))


def solution(mesh):
    replica, nz, ny = (mesh.shape[name] for name in ("replica", "shard", "tensor"))
    fine = Mesh(mesh.devices.reshape(replica // 2, 2, nz, ny), ("x", "core", "shard", "tensor"))
    replicas, rows = ("x", "core"), ("shard", "tensor")
    return jax.shard_map(
        on_device,
        mesh=fine,
        in_specs=(P(replicas, None, rows, None), P(rows, None, replicas, None), P()),
        out_specs=P(None, rows, None),
        check_vma=False,
    )
```
